32 devices in a mesh: aux: 4 (over z), ao: 8 (over y, x, core).
Axes of the slice: x: 2, y: 2, z: 4, core: 2. Of those that a mesh axis runs over, the one named last changes fastest.
Arguments:
- tensor: bfloat16 [64, 1024, 1024], P('aux', 'ao'), may hold values from -6 to 6
- green: bfloat16 [1024, 1024], P('aux', 'ao'), may hold values from -0.1875 to 0.1875
- tensor_mask: int32 [4, 8, 8], P('aux', 'ao'), may hold values 0 or 1
- green_mask: int32 [8, 8], P('aux', 'ao'), may hold values 0 or 1
Outputs:
- contracted: bfloat16 [64, 1024, 1024], P('aux', 'ao')
- polar: float32 [64, 16], P('aux')
The draws below stay inside these ranges and needn't reach their ends.
All inputs are finite; a program needn't handle non-finite values. No bound on the sum of `tensor_mask` or of `green_mask` on one device may be relied on, other than what follows from the above.
Results may differ from the reference program's by a relative error of at most 0.001.
Values may be sent and summed in bfloat16 or wider, within the bound.
A program may use at most 128 MiB of HBM per device.

```python
import jax
import jax.numpy as jnp
from jax import lax

BLK = 128
AUX_DEV = 16
NB = 8
NAO = 1024
NAUX = 64
N_AUX = 4


def plant(result, rng, smallest, largest):
    longest = result.shape.index(max(result.shape))
    spots = []
    for shift in (0, 1):
        where = [jax.random.randint(jax.random.fold_in(rng, axis), (), 0, length) for axis, length in enumerate(result.shape)]
        where[longest] = (where[longest] + shift) % result.shape[longest]
        spots.append(tuple(where))
    return result.at[spots[0]].set(smallest).at[spots[1]].set(largest)


def steps_of(key, extent, cuts, smallest, high):
    def one(dim, shards_of):
        heights = jax.random.uniform(jax.random.fold_in(jax.random.fold_in(key, 6), dim), (shards_of,), jnp.float32, smallest / len(cuts), high / len(cuts))
        return jnp.repeat(jnp.exp(heights), extent[dim] // shards_of).reshape((-1,) + (1,) * (len(extent) - dim - 1))

    loudness = one(*cuts[0])
    for cut in cuts[1:]:
        loudness = loudness * one(*cut)
    return loudness


def noise(rng, extent, spread, reach, cuts=(), held_as=jnp.bfloat16):
    entries = spread * jax.random.normal(rng, extent, jnp.float32)
    if cuts:
        entries = entries * steps_of(rng, extent, cuts, -0.22, 0.18)
    return jnp.clip(entries, -reach, reach).astype(held_as)


def setup_inputs(seed: int = 0) -> dict:
    streams_of = jax.random.split(jax.random.key(seed), 5)
    tensor = noise(streams_of[0], (NAUX, NAO, NAO), 1.0, 6.0, ((0, 4), (1, 8)))
    green = noise(streams_of[1], (NAO, NAO), NAO ** -0.5, 0.1875, ((0, 4), (1, 8)))
    tensor_mask = plant((jax.random.randint(streams_of[2], (N_AUX, NB, NB), 0, 4) < 3).astype(jnp.int32), jax.random.fold_in(streams_of[2], 1), 0, 1)
    green_mask = plant((jax.random.randint(streams_of[3], (NB, NB), 0, 4) < 3).astype(jnp.int32), jax.random.fold_in(streams_of[3], 1), 0, 1)
    return dict(tensor=tensor, green=green, tensor_mask=tensor_mask, green_mask=green_mask)


def expand_blocks(mask, width):
    return jnp.repeat(jnp.repeat(mask, width, axis=0), width, axis=1)


def reference(tensor, green, tensor_mask, green_mask):
    green_used = green * expand_blocks(green_mask, BLK).astype(jnp.bfloat16)
    green_wide = green_used.astype(jnp.float32)
    shards = tensor.reshape(N_AUX, AUX_DEV, NAO, NAO)

    def one_shard(pair):
        block, mask = pair
        masked = (block * expand_blocks(mask, BLK).astype(jnp.bfloat16)[None]).astype(jnp.float32)
        product = jnp.einsum('pmn,nk->pmk', masked, green_wide, precision=lax.Precision.HIGHEST)
        polar = jnp.einsum('pmk,qmk->pq', product, masked, precision=lax.Precision.HIGHEST) / NAO
        return product.astype(jnp.bfloat16), polar

    products, polars = lax.map(one_shard, (shards, tensor_mask))
    return products.reshape(NAUX, NAO, NAO), polars.reshape(NAUX, AUX_DEV)
```

```python
import functools

import jax
import jax.numpy as jnp
from jax import lax
from jax.experimental import pallas as pl
from jax.experimental.pallas import tpu as pltpu
from jax.sharding import PartitionSpec as P

BLK = 128
MESH = pl.DeviceIdType.MESH
TRANS_B = (((1,), (1,)), ((), ()))


def kernel(n_aux, n_ao, tensor_mask, green_mask, tensor, green, contracted, polar,
           g, rhs, tbuf, cbuf, diag, pbuf, t_sem, c_sem, send_sem, recv_sem, psend_sem, precv_sem):
    aux_count, row_count, orbitals = tbuf.shape
    depth = green.shape[0]
    n_chip = n_ao // 2
    a = lax.axis_index("aux")
    o = lax.axis_index("ao")
    chip, core = o // 2, o % 2
    sibling = chip * 2 + 1 - core

    def aux_at(k):
        return (a + k) % n_aux

    if n_chip == 4:
        cx, cy = chip % 2, chip // 2
        chips = [chip, cy * 2 + 1 - cx, (1 - cy) * 2 + cx, (1 - cy) * 2 + 1 - cx]
    else:
        chips = [(chip + t) % n_chip for t in range(n_chip)]
    cols = [c * 2 + core for c in chips]

    load = pltpu.make_async_copy(tensor, tbuf, t_sem)
    load.start()

    barrier = pltpu.get_barrier_semaphore()
    for k in range(1, n_aux):
        pl.semaphore_signal(barrier, inc=1, device_id=(aux_at(k), o), device_id_type=MESH)
    for k in range(1, n_ao):
        pl.semaphore_signal(barrier, inc=1, device_id=(a, (o + k) % n_ao), device_id_type=MESH)

    def piece(pa, po):
        return g.at[pl.ds(pl.multiple_of(pa * depth, depth), depth), pl.ds(pl.multiple_of(po * BLK, BLK), BLK)]

    for b in range(depth // BLK):
        keep = jnp.full((BLK, BLK), green_mask[b, 0].astype(jnp.float32)).astype(jnp.bfloat16)
        rows = pl.ds(pl.multiple_of(a * depth + b * BLK, BLK), BLK)
        g[rows, pl.ds(pl.multiple_of(o * BLK, BLK), BLK)] = green[b * BLK:(b + 1) * BLK, :] * keep
    pl.semaphore_wait(barrier, n_aux - 1 + n_ao - 1)

    sends = []

    def send(pa, po, to):
        copy = pltpu.make_async_remote_copy(
            src_ref=piece(pa, po), dst_ref=piece(pa, po),
            send_sem=send_sem.at[len(sends)], recv_sem=recv_sem.at[pa, po],
            device_id=to, device_id_type=MESH,
        )
        copy.start()
        sends.append(copy)

    def arrived(pa, po):
        pltpu.make_async_remote_copy(
            src_ref=piece(pa, po), dst_ref=piece(pa, po),
            send_sem=send_sem.at[0], recv_sem=recv_sem.at[pa, po],
            device_id=(a, sibling), device_id_type=MESH,
        ).wait_recv()

    def to_chips(k):
        direct = 3 if n_chip == 4 else n_chip
        for t in range(1, direct):
            send(aux_at(k), o, (a, cols[t]))
        send(aux_at(k), o, (a, sibling))

    def forward(k):
        if n_chip == 4:
            first, second = (1, 2) if k % 2 == 0 else (2, 1)
            arrived(aux_at(k), cols[first])
            send(aux_at(k), cols[first], (a, cols[second]))
            send(aux_at(k), cols[first], (a, sibling))
            arrived(aux_at(k), cols[second])
            send(aux_at(k), cols[second], (a, sibling))

    def finish(t, k):
        arrived(aux_at(k), cols[t])
        send(aux_at(k), cols[t], (a, sibling))

    def multiply(t):
        for k in range(n_aux):
            arrived(aux_at(k), chips[t] * 2 + 1 - core)
        lanes = pl.ds(pl.multiple_of(chips[t] * 2 * BLK, 2 * BLK), 2 * BLK)
        for b in range(n_ao):
            keep = jnp.full((BLK, 2 * BLK), tensor_mask[0, 0, b].astype(jnp.float32)).astype(jnp.bfloat16)
            rhs[b * BLK:(b + 1) * BLK, :] = g[b * BLK:(b + 1) * BLK, lanes] * keep
        keep_lanes = jnp.concatenate(
            [jnp.full((16 * aux_count, BLK), tensor_mask[0, 0, chips[t] * 2 + i].astype(jnp.float32)) for i in range(2)],
            axis=1,
        ).astype(jnp.bfloat16)

        def tile(j, carry):
            rows = pl.ds(pl.multiple_of(j * 32, 32), 32)
            left = tbuf[:, rows, :].reshape(aux_count * 32, orbitals)
            product = jnp.dot(left, rhs[...], preferred_element_type=jnp.float32)
            high = product.astype(jnp.bfloat16)
            low = (product - high.astype(jnp.float32)).astype(jnp.bfloat16)
            high = high.reshape(aux_count, 32, 2 * BLK)
            low = low.reshape(aux_count, 32, 2 * BLK)
            cbuf[:, rows, lanes] = high
            right = tbuf[:, rows, lanes]
            total = diag[...]
            for s in range(2):
                part = slice(s * 16, s * 16 + 16)
                kept = right[:, part].reshape(aux_count * 16, 2 * BLK) * keep_lanes
                for half in (high, low):
                    total += lax.dot_general(
                        half[:, part].reshape(aux_count * 16, 2 * BLK), kept, TRANS_B,
                        preferred_element_type=jnp.float32,
                    )
            diag[...] = total
            return carry

        lax.fori_loop(0, row_count // 32, tile, 0)
        store = pltpu.make_async_copy(cbuf.at[:, :, lanes], contracted.at[:, :, lanes], c_sem.at[t])
        store.start()
        return store

    for k in range(1, n_aux):
        send(a, o, (aux_at(k), o))
    to_chips(0)
    diag[...] = jnp.zeros_like(diag)
    for k in range(1, n_aux):
        arrived(aux_at(k), o)
        to_chips(k)
        forward(k - 1)
    load.wait()
    stores = [multiply(0)]
    forward(n_aux - 1)
    for t in range(1, n_chip):
        ahead = [t + 1] if n_chip == 4 else [t]
        for late in ahead:
            if n_chip != 4 or late == 3:
                for k in range(n_aux):
                    finish(late, k)
        stores.append(multiply(t))

    size = 16 * aux_count
    row = lax.broadcasted_iota(jnp.int32, (size, size), 0)
    col = lax.broadcasted_iota(jnp.int32, (size, size), 1)
    same = jnp.where(row % 16 == col % 16, diag[...], 0.0)
    by_row = jnp.sum(same.reshape(aux_count, 16, size), axis=1)
    spread = lax.broadcasted_iota(jnp.int32, (size, BLK), 0) // 16 == lax.broadcasted_iota(jnp.int32, (size, BLK), 1)
    pbuf[o] = jnp.dot(by_row, spread.astype(jnp.float32), precision=lax.Precision.HIGHEST,
                      preferred_element_type=jnp.float32)
    swaps = []
    for k in range(1, n_ao):
        swap = pltpu.make_async_remote_copy(
            src_ref=pbuf.at[o], dst_ref=pbuf.at[o],
            send_sem=psend_sem.at[k], recv_sem=precv_sem.at[o],
            device_id=(a, (o + k) % n_ao), device_id_type=MESH,
        )
        swap.start()
        swaps.append(swap)
    for copy in sends:
        copy.wait_send()
    for store in stores:
        store.wait()
    for k in range(1, n_ao):
        other = (o + k) % n_ao
        pltpu.make_async_remote_copy(
            src_ref=pbuf.at[other], dst_ref=pbuf.at[other],
            send_sem=psend_sem.at[k], recv_sem=precv_sem.at[other],
            device_id=(a, other), device_id_type=MESH,
        ).wait_recv()
    for swap in swaps:
        swap.wait_send()
    whole = pbuf[0]
    for i in range(1, n_ao):
        whole += pbuf[i]
    polar[...] = whole[:, :aux_count] * (1.0 / orbitals)


def local(n_aux, n_ao, tensor, green, tensor_mask, green_mask):
    aux_count, row_count, orbitals = tensor.shape
    bf16, f32 = jnp.bfloat16, jnp.float32
    n_chip = n_ao // 2
    n_sends = n_aux - 1 + n_aux * ((n_chip - 1) + n_chip)
    dma = pltpu.SemaphoreType.DMA
    return pl.pallas_call(
        functools.partial(kernel, n_aux, n_ao),
        out_shape=(
            jax.ShapeDtypeStruct(tensor.shape, bf16),
            jax.ShapeDtypeStruct((aux_count, aux_count), f32),
        ),
        in_specs=[
            pl.BlockSpec(memory_space=pltpu.SMEM),
            pl.BlockSpec(memory_space=pltpu.SMEM),
            pl.BlockSpec(memory_space=pl.ANY),
            pl.BlockSpec(memory_space=pltpu.VMEM),
        ],
        out_specs=(pl.BlockSpec(memory_space=pl.ANY), pl.BlockSpec(memory_space=pltpu.VMEM)),
        scratch_shapes=[
            pltpu.VMEM((orbitals, orbitals), bf16),
            pltpu.VMEM((orbitals, 2 * BLK), bf16),
            pltpu.VMEM(tensor.shape, bf16),
            pltpu.VMEM(tensor.shape, bf16),
            pltpu.VMEM((16 * aux_count, 16 * aux_count), f32),
            pltpu.VMEM((n_ao, aux_count, BLK), f32),
            dma(()),
            dma((n_chip,)),
            dma((n_sends,)),
            dma((n_aux, n_ao)),
            dma((n_ao,)),
            dma((n_ao,)),
        ],
        compiler_params=pltpu.CompilerParams(
            collective_id=0, has_side_effects=True, vmem_limit_bytes=48 * 2**20
        ),
    )(tensor_mask, green_mask, tensor, green)


def solution(mesh):
    return jax.shard_map(
        functools.partial(local, mesh.shape["aux"], mesh.shape["ao"]),
        mesh=mesh,
        in_specs=(P("aux", "ao", None), P("aux", "ao"), P("aux", "ao", None), P("aux", "ao")),
        out_specs=(P("aux", "ao", None), P("aux", None)),
        check_vma=False,
    )
```

```python
import functools

import jax
import jax.numpy as jnp
from jax import lax
from jax.experimental import pallas as pl
from jax.experimental.pallas import tpu as pltpu
from jax.sharding import PartitionSpec as P

BLK = 128
TILE = 64
MESH = pl.DeviceIdType.MESH
TRANS_B = (((1,), (1,)), ((), ()))


def kernel(n_aux, n_ao, tensor_mask, green_mask, tensor, green, contracted, polar,
           g, rhs, tbuf, diag, pbuf, own, g_mask, t_mask, lane_mask, t_sem, in_sem, send_sem, recv_sem, psend_sem, precv_sem):
    aux_count, row_count, orbitals = tbuf.shape
    depth = green.shape[0]
    n_chip = n_ao // 2
    a = lax.axis_index("aux")
    o = lax.axis_index("ao")
    chip, core = o // 2, o % 2
    sibling = chip * 2 + 1 - core

    short = jnp.minimum(a, n_aux - 1 - a)
    from_left = [None] + [jnp.where(k <= 2 * short, k % 2, (2 * a >= n_aux).astype(jnp.int32)) for k in range(1, n_aux)]
    pieces = [a] + [
        a + jnp.where(k <= 2 * short, (k + 1) // 2, k - short) * (1 - 2 * from_left[k]) for k in range(1, n_aux)
    ]

    def aux_at(k):
        return pieces[k]

    if n_chip == 4:
        cx, cy = chip % 2, chip // 2
        chips = [chip, cy * 2 + 1 - cx, (1 - cy) * 2 + cx, (1 - cy) * 2 + 1 - cx]
    else:
        chips = [(chip + t) % n_chip for t in range(n_chip)]
    cols = [c * 2 + core for c in chips]

    load = pltpu.make_async_copy(tensor, tbuf, t_sem)
    loads = [
        pltpu.make_async_copy(green, own, in_sem.at[0]),
        pltpu.make_async_copy(green_mask, g_mask, in_sem.at[1]),
        pltpu.make_async_copy(tensor_mask, t_mask, in_sem.at[2]),
    ]
    for copy in loads:
        copy.start()
    load.start()

    barrier = pltpu.get_barrier_semaphore()
    for k in range(1, n_aux):
        pl.semaphore_signal(barrier, inc=1, device_id=(aux_at(k), o), device_id_type=MESH)
    for k in range(1, n_ao):
        pl.semaphore_signal(barrier, inc=1, device_id=(a, (o + k) % n_ao), device_id_type=MESH)

    def piece(pa, po):
        return g.at[po, pl.ds(pl.multiple_of(pa * depth, depth), depth), :]

    for copy in loads:
        copy.wait()
    for b in range(depth // BLK):
        keep = jnp.broadcast_to(g_mask[b:b + 1, 0:1].astype(jnp.float32), (BLK, BLK)).astype(jnp.bfloat16)
        rows = pl.ds(pl.multiple_of(a * depth + b * BLK, BLK), BLK)
        g[o, rows, :] = own[b * BLK:(b + 1) * BLK, :] * keep
    for b in range(n_ao):
        lane_mask[:, b * BLK:(b + 1) * BLK] = jnp.broadcast_to(
            t_mask[0, 0:1, b:b + 1].astype(jnp.float32), lane_mask[:, b * BLK:(b + 1) * BLK].shape
        )
    pl.semaphore_wait(barrier, n_ao - 1 + n_aux - 1)

    sends = []

    def send(pa, po, to):
        copy = pltpu.make_async_remote_copy(
            src_ref=piece(pa, po), dst_ref=piece(pa, po),
            send_sem=send_sem.at[len(sends)], recv_sem=recv_sem.at[pa, po],
            device_id=to, device_id_type=MESH,
        )
        copy.start()
        sends.append(copy)

    def arrived(pa, po):
        pltpu.make_async_remote_copy(
            src_ref=piece(pa, po), dst_ref=piece(pa, po),
            send_sem=send_sem.at[0], recv_sem=recv_sem.at[pa, po],
            device_id=(a, sibling), device_id_type=MESH,
        ).wait_recv()

    cross = n_chip == 4

    def to_chips(k):
        for t in range(1, 3 if cross and k > 0 else n_chip):
            send(aux_at(k), o, (a, cols[t]))
        send(aux_at(k), o, (a, sibling))

    def finish(t, k):
        arrived(aux_at(k), cols[t])
        send(aux_at(k), cols[t], (a, sibling))

    def multiply(t):
        for k in range(n_aux):
            arrived(aux_at(k), chips[t] * 2 + 1 - core)
        lanes = pl.ds(pl.multiple_of(chips[t] * 2 * BLK, 2 * BLK), 2 * BLK)
        for b in range(n_ao):
            keep = jnp.broadcast_to(lane_mask[0:1, b * BLK:b * BLK + 1], (BLK, BLK)).astype(jnp.bfloat16)
            for i in range(2):
                rhs[b * BLK:(b + 1) * BLK, i * BLK:(i + 1) * BLK] = g[chips[t] * 2 + i, b * BLK:(b + 1) * BLK, :] * keep
        keep_lanes = jnp.broadcast_to(lane_mask[0:1, lanes], (16 * aux_count, 2 * BLK)).astype(jnp.bfloat16)

        def tile(j, carry):
            rows = pl.ds(pl.multiple_of(j * TILE, TILE), TILE)
            left_rows = tbuf[:, rows, :].reshape(aux_count * TILE, orbitals)
            product = jnp.dot(left_rows, rhs[...], preferred_element_type=jnp.float32)
            high = product.astype(jnp.bfloat16)
            low = (product - high.astype(jnp.float32)).astype(jnp.bfloat16)
            high = high.reshape(aux_count, TILE, 2 * BLK)
            low = low.reshape(aux_count, TILE, 2 * BLK)
            contracted[:, rows, lanes] = high
            right_rows = tbuf[:, rows, lanes]
            total = diag[...]
            for s in range(TILE // 16):
                part = slice(s * 16, s * 16 + 16)
                kept = right_rows[:, part].reshape(aux_count * 16, 2 * BLK) * keep_lanes
                halves = jnp.concatenate([high[:, part], low[:, part]], axis=0).reshape(aux_count * 32, 2 * BLK)
                total += lax.dot_general(halves, kept, TRANS_B, preferred_element_type=jnp.float32)
            diag[...] = total
            return carry

        lax.fori_loop(0, row_count // TILE, tile, 0)

    for k in range(1, n_aux):
        send(a, o, (aux_at(k), o))
    to_chips(0)
    diag[...] = jnp.zeros_like(diag)
    if cross:
        finish(3, 0)
        for k in range(1, n_aux):
            send(a, cols[3], (aux_at(k), o))
    for k in range(1, n_aux):
        arrived(aux_at(k), o)
        to_chips(k)
    load.wait()
    multiply(0)
    for t in range(1, n_chip):
        if cross and t == 1:
            for late in (1, 2):
                for k in range(n_aux):
                    finish(late, k)
        if cross and t == 2:
            for k in range(1, n_aux):
                finish(3, k)
        if not cross:
            for k in range(n_aux):
                finish(t, k)
        multiply(t)

    size = 16 * aux_count
    row = lax.broadcasted_iota(jnp.int32, (size, size), 0)
    col = lax.broadcasted_iota(jnp.int32, (size, size), 1)
    same = jnp.where(row % 16 == col % 16, diag[0:size, :] + diag[size:, :], 0.0)
    by_row = jnp.sum(same.reshape(aux_count, 16, size), axis=1)
    spread = lax.broadcasted_iota(jnp.int32, (size, BLK), 0) // 16 == lax.broadcasted_iota(jnp.int32, (size, BLK), 1)
    pbuf[o] = jnp.dot(by_row, spread.astype(jnp.float32), precision=lax.Precision.HIGHEST,
                      preferred_element_type=jnp.float32)
    swaps = []
    for k in range(1, n_ao):
        swap = pltpu.make_async_remote_copy(
            src_ref=pbuf.at[o], dst_ref=pbuf.at[o],
            send_sem=psend_sem.at[k], recv_sem=precv_sem.at[o],
            device_id=(a, (o + k) % n_ao), device_id_type=MESH,
        )
        swap.start()
        swaps.append(swap)
    for copy in sends:
        copy.wait_send()
    for k in range(1, n_ao):
        other = (o + k) % n_ao
        pltpu.make_async_remote_copy(
            src_ref=pbuf.at[other], dst_ref=pbuf.at[other],
            send_sem=psend_sem.at[k], recv_sem=precv_sem.at[other],
            device_id=(a, other), device_id_type=MESH,
        ).wait_recv()
    for swap in swaps:
        swap.wait_send()
    whole = pbuf[0]
    for i in range(1, n_ao):
        whole += pbuf[i]
    polar[...] = whole[:, :aux_count] * (1.0 / orbitals)


def local(n_aux, n_ao, tensor, green, tensor_mask, green_mask):
    aux_count, row_count, orbitals = tensor.shape
    bf16, f32 = jnp.bfloat16, jnp.float32
    n_chip = n_ao // 2
    n_sends = n_aux - 1 + n_aux * ((n_chip - 1) + n_chip)
    dma = pltpu.SemaphoreType.DMA
    return pl.pallas_call(
        functools.partial(kernel, n_aux, n_ao),
        out_shape=(
            jax.ShapeDtypeStruct(tensor.shape, bf16),
            jax.ShapeDtypeStruct((aux_count, aux_count), f32),
        ),
        in_specs=[
            pl.BlockSpec(memory_space=pltpu.HBM),
            pl.BlockSpec(memory_space=pltpu.HBM),
            pl.BlockSpec(memory_space=pltpu.HBM),
            pl.BlockSpec(memory_space=pltpu.HBM),
        ],
        out_specs=(pl.BlockSpec(memory_space=pltpu.VMEM), pl.BlockSpec(memory_space=pltpu.VMEM)),
        scratch_shapes=[
            pltpu.VMEM((n_ao, orbitals, BLK), bf16),
            pltpu.VMEM((orbitals, 2 * BLK), bf16),
            pltpu.VMEM(tensor.shape, bf16),
            pltpu.VMEM((32 * aux_count, 16 * aux_count), f32),
            pltpu.VMEM((n_ao, aux_count, BLK), f32),
            pltpu.VMEM(green.shape, bf16),
            pltpu.VMEM(green_mask.shape, jnp.int32),
            pltpu.VMEM(tensor_mask.shape, jnp.int32),
            pltpu.VMEM((8, orbitals), f32),
            dma(()),
            dma((3,)),
            dma((n_sends,)),
            dma((n_aux, n_ao)),
            dma((n_ao,)),
            dma((n_ao,)),
        ],
        compiler_params=pltpu.CompilerParams(
            collective_id=0, has_side_effects=True, vmem_limit_bytes=48 * 2**20
        ),
    )(tensor_mask, green_mask, tensor, green)


def solution(mesh):
    return jax.shard_map(
        functools.partial(local, mesh.shape["aux"], mesh.shape["ao"]),
        mesh=mesh,
        in_specs=(P("aux", "ao", None), P("aux", "ao"), P("aux", "ao", None), P("aux", "ao")),
        out_specs=(P("aux", "ao", None), P("aux", None)),
        check_vma=False,
    )
```

```python
import functools

import jax
import jax.numpy as jnp
from jax import lax
from jax.experimental import pallas as pl
from jax.experimental.pallas import tpu as pltpu
from jax.sharding import PartitionSpec as P

BLK = 128
TILE = 32
MESH = pl.DeviceIdType.MESH
TRANS_B = (((1,), (1,)), ((), ()))


def kernel(n_aux, n_ao, tensor_mask, green_mask, tensor, green, contracted, polar,
           g, rhs, tbuf, diag, pbuf, own, g_mask, t_mask, lane_mask, t_sem, in_sem, send_sem, recv_sem, psend_sem, precv_sem):
    aux_count, row_count, orbitals = tbuf.shape
    depth = green.shape[0]
    n_chip = n_ao // 2
    a = lax.axis_index("aux")
    o = lax.axis_index("ao")
    chip, core = o // 2, o % 2
    sibling = chip * 2 + 1 - core

    short = jnp.minimum(a, n_aux - 1 - a)
    from_left = [None] + [jnp.where(k <= 2 * short, k % 2, (2 * a >= n_aux).astype(jnp.int32)) for k in range(1, n_aux)]
    pieces = [a] + [
        a + jnp.where(k <= 2 * short, (k + 1) // 2, k - short) * (1 - 2 * from_left[k]) for k in range(1, n_aux)
    ]

    def aux_at(k):
        return pieces[k]

    if n_chip == 4:
        cx, cy = chip % 2, chip // 2
        chips = [chip, cy * 2 + 1 - cx, (1 - cy) * 2 + cx, (1 - cy) * 2 + 1 - cx]
    else:
        chips = [(chip + t) % n_chip for t in range(n_chip)]
    cols = [c * 2 + core for c in chips]

    load = pltpu.make_async_copy(tensor, tbuf, t_sem)
    loads = [
        pltpu.make_async_copy(green, own, in_sem.at[0]),
        pltpu.make_async_copy(green_mask, g_mask, in_sem.at[1]),
        pltpu.make_async_copy(tensor_mask, t_mask, in_sem.at[2]),
    ]
    for copy in loads:
        copy.start()
    load.start()

    barrier = pltpu.get_barrier_semaphore()
    for k in range(1, n_aux):
        pl.semaphore_signal(barrier, inc=1, device_id=(aux_at(k), o), device_id_type=MESH)
    for k in range(1, n_ao):
        pl.semaphore_signal(barrier, inc=1, device_id=(a, (o + k) % n_ao), device_id_type=MESH)

    def piece(pa, po):
        return g.at[po, pl.ds(pl.multiple_of(pa * depth, depth), depth), :]

    for copy in loads:
        copy.wait()
    for b in range(depth // BLK):
        keep = jnp.broadcast_to(g_mask[b:b + 1, 0:1].astype(jnp.float32), (BLK, BLK)).astype(jnp.bfloat16)
        rows = pl.ds(pl.multiple_of(a * depth + b * BLK, BLK), BLK)
        g[o, rows, :] = own[b * BLK:(b + 1) * BLK, :] * keep
    for b in range(n_ao):
        lane_mask[:, b * BLK:(b + 1) * BLK] = jnp.broadcast_to(
            t_mask[0, 0:1, b:b + 1].astype(jnp.float32), lane_mask[:, b * BLK:(b + 1) * BLK].shape
        )
    pl.semaphore_wait(barrier, n_ao - 1 + n_aux - 1)

    sends = []

    def send(pa, po, to):
        copy = pltpu.make_async_remote_copy(
            src_ref=piece(pa, po), dst_ref=piece(pa, po),
            send_sem=send_sem.at[len(sends)], recv_sem=recv_sem.at[pa, po],
            device_id=to, device_id_type=MESH,
        )
        copy.start()
        sends.append(copy)

    def arrived(pa, po):
        pltpu.make_async_remote_copy(
            src_ref=piece(pa, po), dst_ref=piece(pa, po),
            send_sem=send_sem.at[0], recv_sem=recv_sem.at[pa, po],
            device_id=(a, sibling), device_id_type=MESH,
        ).wait_recv()

    cross = n_chip == 4

    def to_chips(k):
        for t in range(1, 3 if cross and k > 0 else n_chip):
            send(aux_at(k), o, (a, cols[t]))
        send(aux_at(k), o, (a, sibling))

    def finish(t, k):
        arrived(aux_at(k), cols[t])
        send(aux_at(k), cols[t], (a, sibling))

    def multiply(t):
        for k in range(n_aux):
            arrived(aux_at(k), chips[t] * 2 + 1 - core)
        lanes = pl.ds(pl.multiple_of(chips[t] * 2 * BLK, 2 * BLK), 2 * BLK)
        for b in range(n_ao):
            keep = jnp.broadcast_to(lane_mask[0:1, b * BLK:b * BLK + 1], (BLK, BLK)).astype(jnp.bfloat16)
            for i in range(2):
                rhs[b * BLK:(b + 1) * BLK, i * BLK:(i + 1) * BLK] = g[chips[t] * 2 + i, b * BLK:(b + 1) * BLK, :] * keep
        keep_lanes = jnp.broadcast_to(lane_mask[0:1, lanes], (16 * aux_count, 2 * BLK)).astype(jnp.bfloat16)

        def tile(j, carry):
            rows = pl.ds(pl.multiple_of(j * TILE, TILE), TILE)
            left_rows = tbuf[:, rows, :].reshape(aux_count * TILE, orbitals)
            product = jnp.dot(left_rows, rhs[...], preferred_element_type=jnp.float32)
            high = product.astype(jnp.bfloat16)
            low = (product - high.astype(jnp.float32)).astype(jnp.bfloat16)
            high = high.reshape(aux_count, TILE, 2 * BLK)
            low = low.reshape(aux_count, TILE, 2 * BLK)
            contracted[:, rows, lanes] = high
            right_rows = tbuf[:, rows, lanes]
            parts = [slice(s * 16, s * 16 + 16) for s in range(TILE // 16)]
            kept = jnp.concatenate(
                [right_rows[:, part].reshape(aux_count * 16, 2 * BLK) * keep_lanes for part in parts], axis=1
            )
            halves = jnp.concatenate(
                [jnp.concatenate([high[:, part], low[:, part]], axis=0).reshape(aux_count * 32, 2 * BLK)
                 for part in parts], axis=1,
            )
            diag[...] += lax.dot_general(halves, kept, TRANS_B, preferred_element_type=jnp.float32)
            return carry

        lax.fori_loop(0, row_count // TILE, tile, 0, unroll=True)

    for k in range(1, n_aux):
        send(a, o, (aux_at(k), o))
    to_chips(0)
    diag[...] = jnp.zeros_like(diag)
    if cross:
        finish(3, 0)
        for k in range(1, n_aux):
            send(a, cols[3], (aux_at(k), o))
    for k in range(1, n_aux):
        arrived(aux_at(k), o)
        to_chips(k)
    load.wait()
    multiply(0)
    for t in range(1, n_chip):
        if cross and t == 1:
            for late in (1, 2):
                for k in range(n_aux):
                    finish(late, k)
        if cross and t == 2:
            for k in range(1, n_aux):
                finish(3, k)
        if not cross:
            for k in range(n_aux):
                finish(t, k)
        multiply(t)

    size = 16 * aux_count
    row = lax.broadcasted_iota(jnp.int32, (size, size), 0)
    col = lax.broadcasted_iota(jnp.int32, (size, size), 1)
    same = jnp.where(row % 16 == col % 16, diag[0:size, :] + diag[size:, :], 0.0)
    by_row = jnp.sum(same.reshape(aux_count, 16, size), axis=1)
    spread = lax.broadcasted_iota(jnp.int32, (size, BLK), 0) // 16 == lax.broadcasted_iota(jnp.int32, (size, BLK), 1)
    pbuf[o] = jnp.dot(by_row, spread.astype(jnp.float32), precision=lax.Precision.HIGHEST,
                      preferred_element_type=jnp.float32)
    swaps = []
    for k in range(1, n_ao):
        swap = pltpu.make_async_remote_copy(
            src_ref=pbuf.at[o], dst_ref=pbuf.at[o],
            send_sem=psend_sem.at[k], recv_sem=precv_sem.at[o],
            device_id=(a, (o + k) % n_ao), device_id_type=MESH,
        )
        swap.start()
        swaps.append(swap)
    for copy in sends:
        copy.wait_send()
    for k in range(1, n_ao):
        other = (o + k) % n_ao
        pltpu.make_async_remote_copy(
            src_ref=pbuf.at[other], dst_ref=pbuf.at[other],
            send_sem=psend_sem.at[k], recv_sem=precv_sem.at[other],
            device_id=(a, other), device_id_type=MESH,
        ).wait_recv()
    for swap in swaps:
        swap.wait_send()
    whole = pbuf[0]
    for i in range(1, n_ao):
        whole += pbuf[i]
    polar[...] = whole[:, :aux_count] * (1.0 / orbitals)


def local(n_aux, n_ao, tensor, green, tensor_mask, green_mask):
    aux_count, row_count, orbitals = tensor.shape
    bf16, f32 = jnp.bfloat16, jnp.float32
    n_chip = n_ao // 2
    n_sends = n_aux - 1 + n_aux * ((n_chip - 1) + n_chip)
    dma = pltpu.SemaphoreType.DMA
    return pl.pallas_call(
        functools.partial(kernel, n_aux, n_ao),
        out_shape=(
            jax.ShapeDtypeStruct(tensor.shape, bf16),
            jax.ShapeDtypeStruct((aux_count, aux_count), f32),
        ),
        in_specs=[
            pl.BlockSpec(memory_space=pltpu.HBM),
            pl.BlockSpec(memory_space=pltpu.HBM),
            pl.BlockSpec(memory_space=pltpu.HBM),
            pl.BlockSpec(memory_space=pltpu.HBM),
        ],
        out_specs=(pl.BlockSpec(memory_space=pltpu.VMEM), pl.BlockSpec(memory_space=pltpu.VMEM)),
        scratch_shapes=[
            pltpu.VMEM((n_ao, orbitals, BLK), bf16),
            pltpu.VMEM((orbitals, 2 * BLK), bf16),
            pltpu.VMEM(tensor.shape, bf16),
            pltpu.VMEM((32 * aux_count, 16 * aux_count), f32),
            pltpu.VMEM((n_ao, aux_count, BLK), f32),
            pltpu.VMEM(green.shape, bf16),
            pltpu.VMEM(green_mask.shape, jnp.int32),
            pltpu.VMEM(tensor_mask.shape, jnp.int32),
            pltpu.VMEM((8, orbitals), f32),
            dma(()),
            dma((3,)),
            dma((n_sends,)),
            dma((n_aux, n_ao)),
            dma((n_ao,)),
            dma((n_ao,)),
        ],
        compiler_params=pltpu.CompilerParams(
            collective_id=0, has_side_effects=True, vmem_limit_bytes=48 * 2**20
        ),
    )(tensor_mask, green_mask, tensor, green)


def solution(mesh):
    return jax.shard_map(
        functools.partial(local, mesh.shape["aux"], mesh.shape["ao"]),
        mesh=mesh,
        in_specs=(P("aux", "ao", None), P("aux", "ao"), P("aux", "ao", None), P("aux", "ao")),
        out_specs=(P("aux", "ao", None), P("aux", None)),
        check_vma=False,
    )
```
